1024 devices in a mesh: tok: 64 (over x_hi, z, core), ten: 16 (over y, x_lo).
Axes of the slice: x: 4 (x_hi: 2, x_lo: 2; x = x_hi * 2 + x_lo), y: 8, z: 16, core: 2. Of those that a mesh axis runs over, the one named last changes fastest.
Arguments:
- counts: int32 [4096, 128256], P('ten', 'tok'), may hold values from 0 to 31
- u_factor: float32 [64, 4096], P('tok', 'ten'), may hold values from -2.5 to 2.5
- u_accum: float32 [64, 4096], P('tok', 'ten'), may hold values from 8016 to 513024
- v_factor: float32 [64, 128256], P('ten', 'tok'), may hold values from -2.5 to 2.5
- v_accum: float32 [64, 128256], P('ten', 'tok'), may hold values from 256 to 16384
Outputs:
- u_next: float32 [64, 4096], P('tok', 'ten')
- u_accum_next: float32 [64, 4096], P('tok', 'ten')
- v_next: float32 [64, 128256], P('ten', 'tok')
- v_accum_next: float32 [64, 128256], P('ten', 'tok')
The draws below stay inside these ranges and needn't reach their ends.
All inputs are finite; a program needn't handle non-finite values.
Results may differ from the reference program's by a relative error of at most 0.0076.
Values may be sent and summed in bfloat16 or wider, within the bound.
A program may use at most 32 MiB of HBM per device.

```python
import math
import jax
import jax.numpy as jnp
import numpy as np
from jax import lax

RANK = 64
VOCAB = 128256
TEN_DEV = 256
TENANTS = 4096


def place_ends(values, stream_key, smallest, high):
    shape = values.shape
    index_at = [jax.random.randint(jax.random.fold_in(stream_key, axis), (), 0, shape[axis]) for axis in range(len(shape))]
    values = values.at[tuple(index_at)].set(smallest)
    longest = shape.index(max(shape))
    index_at[longest] = (index_at[longest] + 1) % shape[longest]
    return values.at[tuple(index_at)].set(high)


def strengthened(drawn, rng, source, target, shards_of, factor):
    owner, partner = [(jnp.arange(drawn.shape[dim]) // (drawn.shape[dim] // shards_of)).reshape([-1 if axis == dim else 1 for axis in range(drawn.ndim)]) for dim in (source, target)]
    chosen = jax.random.permutation(rng, shards_of)[partner]
    strong = (owner == chosen) | (owner == (partner + shards_of // 2) % shards_of)
    return jnp.where(strong, factor * drawn, drawn)


def steps_of(stream_key, dims, shards, smallest, top_value):
    loudness, own = 1.0, jax.random.fold_in(stream_key, 6)
    for position, shards_of in shards:
        draws = jnp.exp(jax.random.uniform(jax.random.fold_in(own, position), (shards_of,), jnp.float32, smallest / len(shards), top_value / len(shards)))
        loudness = loudness * jnp.repeat(draws, dims[position] // shards_of).reshape([-1 if axis == position else 1 for axis in range(len(dims))])
    return loudness


def cumulative_ranks(count, slope):
    weights = [(1 << 20) // math.isqrt(rank ** slope) + 1 for rank in range(1, count + 1)]
    deviation = 1 + sum(weights) // (1 << 30)
    return np.cumsum(np.array([max(1, weight // deviation) for weight in weights]))


def ranked(stream_key, shape, number_of, skew):
    grid = cumulative_ranks(number_of, skew)
    lot = jax.random.randint(jax.random.fold_in(stream_key, 1), shape, 0, int(grid[number_of - 1]))
    grade = jnp.searchsorted(jnp.asarray(grid, jnp.int32), lot, side="right")
    return jax.random.permutation(jax.random.fold_in(stream_key, 2), number_of)[grade].astype(jnp.int32)


def noise_with(key, shape, width, bound, split, heavy, held_as=jnp.bfloat16):
    result = width * jax.random.normal(key, shape, jnp.float32)
    if split:
        result = result * steps_of(key, shape, split, -0.22, 0.18)
    return jnp.clip(strengthened(result, jax.random.fold_in(key, 3), *heavy), -bound, bound).astype(held_as)


def setup_inputs(seed: int = 0) -> dict:
    key_list = jax.random.split(jax.random.key(seed), 6)
    counts = place_ends(ranked(key_list[0], (TENANTS, VOCAB), 32, 2), jax.random.fold_in(key_list[0], 3), 0, 31).astype(jnp.int32)
    u_factor = noise_with(key_list[1], (RANK, TENANTS), 0.35, 2.5, ((0, 64), (1, 16)), (1, 0, 64, 4.0), jnp.float32)
    u_accum = jnp.clip(jnp.exp(math.log(513024.0) - 4.158883 * jax.random.uniform(key_list[2], (RANK, TENANTS), jnp.float32) ** steps_of(key_list[2], (RANK, TENANTS), ((0, 64), (1, 16)), -0.2, 0.2)), 8016.0, 513024.0)
    v_factor = noise_with(key_list[3], (RANK, VOCAB), 0.35, 2.5, ((0, 16), (1, 64)), (1, 0, 64, 4.0), jnp.float32)
    v_accum = jnp.clip(jnp.exp(math.log(16384.0) - 4.158883 * jax.random.uniform(key_list[4], (RANK, VOCAB), jnp.float32) ** steps_of(key_list[4], (RANK, VOCAB), ((0, 16), (1, 64)), -0.2, 0.2)), 256.0, 16384.0)
    return dict(counts=counts, u_factor=u_factor, u_accum=u_accum, v_factor=v_factor, v_accum=v_accum)


weight_scale = 0.5
step_rate = 0.3

def residual(low_block, v_low, count_block):
    logits = jnp.dot(low_block.T, v_low, preferred_element_type=jnp.float32)
    weighted = weight_scale * count_block.astype(jnp.float32)
    return (weighted - (1.0 + weighted) * jax.nn.sigmoid(logits)).astype(jnp.bfloat16)

def reference(counts, u_factor, u_accum, v_factor, v_accum):
    blocks = TENANTS // TEN_DEV
    u_low = u_factor.astype(jnp.bfloat16)
    v_low = v_factor.astype(jnp.bfloat16)
    count_blocks = counts.reshape(blocks, TEN_DEV, VOCAB)
    u_blocks = u_low.reshape(RANK, blocks, TEN_DEV).transpose(1, 0, 2)

    def grad_block(pair):
        low_block, count_block = pair
        resid = residual(low_block, v_low, count_block)
        return jnp.dot(v_low, resid.T, preferred_element_type=jnp.float32)
    grads = lax.map(grad_block, (u_blocks, count_blocks))
    grad_u = grads.transpose(1, 0, 2).reshape(RANK, TENANTS)
    u_accum_next = u_accum + grad_u * grad_u
    u_next = u_factor + step_rate * grad_u / jnp.sqrt(u_accum_next)
    fresh_blocks = u_next.astype(jnp.bfloat16).reshape(RANK, blocks, TEN_DEV).transpose(1, 0, 2)

    def add_block(total, pair):
        low_block, count_block = pair
        resid = residual(low_block, v_low, count_block)
        return (total + jnp.dot(low_block, resid, preferred_element_type=jnp.float32), None)
    grad_v, _ = lax.scan(add_block, jnp.zeros((RANK, VOCAB), jnp.float32), (fresh_blocks, count_blocks))
    v_accum_next = v_accum + grad_v * grad_v
    v_next = v_factor + step_rate * grad_v / jnp.sqrt(v_accum_next)
    return (u_next, u_accum_next, v_next, v_accum_next)
```

```python
import jax
import jax.numpy as jnp
from jax import lax
from jax.experimental import pallas as pl
from jax.experimental.pallas import tpu as pltpu
from jax.sharding import PartitionSpec as P

MESH = pl.DeviceIdType.MESH
step_rate = 0.3
RANK = 64
TEN_DEV = 256
TOK_DEV = 2004
PAD = 2048
CHUNK = 512
CHUNKS = PAD // CHUNK
f32, bf16 = jnp.float32, jnp.bfloat16


def place():
    tok, ten = lax.axis_index("tok"), lax.axis_index("ten")
    return tok // 32, (tok // 2) % 16, tok % 2, ten // 2, ten % 2


def tok_at(half, z, core):
    return {"tok": half * 32 + z * 2 + core}


def far_first(step, size):
    return size // 2 + ((step + 1) // 2) * (1 - 2 * (step % 2))


def each_z(body):
    _, z, _, _, _ = place()

    def one(step, carry):
        body((z + far_first(step, 16)) % 16)
        return carry

    lax.fori_loop(0, 15, one, 0)


def each_quad(body):
    half, _, core, _, _ = place()
    for dh, dc in ((1, 1), (1, 0), (0, 1)):
        body((half + dh) % 2, (core + dc) % 2)


def each_tok(body):
    half, z, core, _, _ = place()

    def one(step, carry):
        peer_z = (z + far_first(step, 16)) % 16
        for dh, dc in ((1, 1), (1, 0), (0, 1), (0, 0)):
            body((half + dh) % 2, peer_z, (core + dc) % 2)
        return carry

    lax.fori_loop(0, 15, one, 0)
    each_quad(lambda h, c: body(h, z, c))


def each_ten(body):
    _, _, _, y, x = place()

    def one(step, carry):
        peer_y = (y + far_first(step, 8)) % 8
        for dx in (1, 0):
            body(peer_y * 2 + (x + dx) % 2)
        return carry

    lax.fori_loop(0, 7, one, 0)
    body(y * 2 + (x + 1) % 2)


def send(src, dst, sems, phase, peer):
    send_sem, recv_sem = sems
    pltpu.make_async_remote_copy(
        src_ref=src,
        dst_ref=dst,
        send_sem=send_sem.at[phase],
        recv_sem=recv_sem.at[phase],
        device_id=peer,
        device_id_type=MESH,
    ).start()


def wait_bytes(like, sem):
    pltpu.make_async_copy(like, like, sem).wait()


def kernel(
    counts, u_factor, u_accum, v_factor, v_accum,
    u_next, u_accum_next, v_next, v_accum_next,
    cnt, weight, u_in, ua_in, v_in, va_in, v_rows, u_row, ua_row,
    v_all, v_ranks, v_half, order, u_all, ua_all,
    gu_out, gu_in, gu_z, u_rows, fresh, gv_out, gv_in, gv_sum, g_tile,
    local_sem, send_sem, recv_sem,
):
    half, z, core, y, x = place()
    ten = y * 2 + x
    quad = half * 2 + core
    slot = quad * 16 + z
    sems = (send_sem, recv_sem)

    loads = [
        pltpu.make_async_copy(src, dst, local_sem.at[i])
        for i, (src, dst) in enumerate(
            ((v_factor, v_in), (u_factor, u_in), (u_accum, ua_in), (v_accum, va_in))
        )
    ]
    for q in range(CHUNKS):
        rows = pl.ds(q * CHUNK, min(CHUNK, TOK_DEV - q * CHUNK))
        loads.append(pltpu.make_async_copy(counts.at[rows], cnt.at[rows], local_sem.at[4 + q]))
    for load in loads:
        load.start()

    barrier = pltpu.get_barrier_semaphore()

    def greet(peer):
        pl.semaphore_signal(barrier, inc=1, device_id=peer, device_id_type=MESH)

    each_tok(lambda h, pz, c: greet(tok_at(h, pz, c)))
    each_ten(lambda peer: greet({"ten": peer}))

    v_rows[60:64, :] = jnp.zeros((4, 128), f32)
    loads[0].wait()
    for b in range(16):
        width = min(128, TOK_DEV - b * 128)
        v_rows[4 * b : 4 * b + 4, :width] = v_in[:, b * 128 : b * 128 + width]
    v_all[ten] = v_rows[...].astype(bf16)
    loads[1].wait()
    loads[2].wait()
    for b in range(2):
        u_row[b : b + 1, :] = u_in[:, b * 128 : b * 128 + 128]
        ua_row[b : b + 1, :] = ua_in[:, b * 128 : b * 128 + 128]
    u_all[slot] = u_row[...]
    ua_all[z] = ua_row[...]

    pl.semaphore_wait(barrier, 78)

    each_tok(lambda h, pz, c: send(u_row, u_all.at[slot], sems, 0, tok_at(h, pz, c)))
    each_ten(lambda peer: send(v_all.at[ten], v_all.at[ten], sems, 2, {"ten": peer}))
    each_z(lambda pz: send(ua_row, ua_all.at[z], sems, 1, tok_at(half, pz, core)))

    row = lax.broadcasted_iota(jnp.int32, (256, 256), 0)
    col = lax.broadcasted_iota(jnp.int32, (256, 256), 1)
    rank = (row >> 4) * 4 + (row & 3)
    col_rank = (col & 32) + (col & 15) * 2 + ((col >> 4) & 1)
    same = (((row >> 2) & 3) == (col >> 6)) & (rank == col_rank)
    order[...] = jnp.where(same, 1.0, 0.0).astype(bf16)

    weight[PAD - 48 :, :] = jnp.zeros((48, TEN_DEV), bf16)
    for q in range(CHUNKS):
        loads[4 + q].wait()
        rows = slice(q * CHUNK, min(q * CHUNK + CHUNK, TOK_DEV))
        weight[rows, :] = (0.5 + 0.25 * cnt[rows, :].astype(f32)).astype(bf16)

    wait_bytes(v_all.at[pl.ds(0, 15)], recv_sem.at[2])
    for q in range(CHUNKS):
        block = v_all[:, 16 * q : 16 * q + 16, :].reshape(256, 128)
        ranks = lax.dot_general(
            order[...], block, (((0,), (0,)), ((), ())), preferred_element_type=f32
        )
        for b in range(4):
            start = q * CHUNK + b * 128
            v_ranks[:, start : start + 128] = ranks[64 * b : 64 * b + 64, :].astype(bf16)
            v_half[start : start + 128, :] = (0.5 * ranks[64 * b : 64 * b + 64, :]).T.astype(bf16)

    def residual(low, q):
        rows = slice(q * CHUNK, (q + 1) * CHUNK)
        t = jnp.tanh(jnp.dot(v_half[rows, :], low, preferred_element_type=f32))
        return (weight[rows, :].astype(f32) * (1.0 - t) - 1.0).astype(bf16)

    wait_bytes(u_all.at[pl.ds(0, 63)], recv_sem.at[0])
    u_full = jnp.concatenate([u_all[:, 0, :], u_all[:, 1, :]], axis=1)
    low = u_full.astype(bf16)
    grad_u = jnp.zeros((RANK, TEN_DEV), f32)
    for q in range(CHUNKS):
        grad_u += jnp.dot(
            v_ranks[:, q * CHUNK : (q + 1) * CHUNK], residual(low, q), preferred_element_type=f32
        )
    gu_out[...] = grad_u.reshape(4, 16, TEN_DEV)

    each_quad(lambda h, c: send(gu_out.at[h * 2 + c], gu_in.at[quad], sems, 3, tok_at(h, z, c)))
    gu_in[quad] = gu_out[quad]
    wait_bytes(gu_in.at[pl.ds(0, 3)], recv_sem.at[3])
    gu_z[z] = ((gu_in[0] + gu_in[1]) + (gu_in[2] + gu_in[3])).astype(bf16)
    each_z(lambda pz: send(gu_z.at[z], gu_z.at[z], sems, 4, tok_at(half, pz, core)))
    wait_bytes(ua_all.at[pl.ds(0, 15)], recv_sem.at[1])
    mine = u_all[pl.ds(quad * 16, 16)]
    factor = jnp.concatenate([mine[:, 0, :], mine[:, 1, :]], axis=1)
    accum = jnp.concatenate([ua_all[:, 0, :], ua_all[:, 1, :]], axis=1)
    wait_bytes(gu_z.at[pl.ds(0, 15)], recv_sem.at[4])
    grad = jnp.sum(gu_z[...].astype(f32), axis=0)
    accum = accum + grad * grad
    factor = factor + step_rate * grad / jnp.sqrt(accum)
    fresh[quad] = factor.astype(bf16)
    each_quad(lambda h, c: send(fresh.at[quad], fresh.at[quad], sems, 5, tok_at(h, z, c)))
    u_rows[0] = factor
    u_rows[1] = accum
    u_next[...] = u_rows[0, pl.ds(z, 1), :]
    u_accum_next[...] = u_rows[1, pl.ds(z, 1), :]
    wait_bytes(fresh.at[pl.ds(0, 3)], recv_sem.at[5])

    low = fresh[...].reshape(RANK, TEN_DEV)
    for q in range(CHUNKS):
        part = lax.dot_general(
            low, residual(low, q), (((1,), (1,)), ((), ())), preferred_element_type=f32
        ).astype(bf16)
        stacked = jnp.concatenate([part[:, 128 * b : 128 * b + 128] for b in range(4)], axis=0)
        pieces = jnp.dot(order[...], stacked, preferred_element_type=f32).astype(bf16)
        gv_out[q] = pieces.reshape(16, 16, 128)
        each_ten(lambda peer: send(gv_out.at[q, peer], gv_in.at[q, ten], sems, 6 + q, {"ten": peer}))
        gv_in[q, ten] = gv_out[q, ten]

    loads[3].wait()
    for q in range(CHUNKS):
        wait_bytes(gv_in.at[q, pl.ds(0, 15)], recv_sem.at[6 + q])
        gv_sum[...] = jnp.sum(gv_in[q].astype(f32), axis=0)
        for b in range(4):
            start = q * CHUNK + b * 128
            g_tile[:, start : start + 128] = gv_sum[4 * b : 4 * b + 4, :]
    grad = g_tile[:, :TOK_DEV]
    accum = va_in[...] + grad * grad
    v_accum_next[...] = accum
    v_next[...] = v_in[...] + step_rate * grad / jnp.sqrt(accum)

    wait_bytes(u_all.at[pl.ds(0, 63)], send_sem.at[0])
    wait_bytes(ua_all.at[pl.ds(0, 15)], send_sem.at[1])
    wait_bytes(v_all.at[pl.ds(0, 15)], send_sem.at[2])
    wait_bytes(gu_in.at[pl.ds(0, 3)], send_sem.at[3])
    wait_bytes(gu_z.at[pl.ds(0, 15)], send_sem.at[4])
    wait_bytes(fresh.at[pl.ds(0, 3)], send_sem.at[5])
    for q in range(CHUNKS):
        wait_bytes(gv_in.at[q, pl.ds(0, 15)], send_sem.at[6 + q])


def store(*refs):
    copies = [
        pltpu.make_async_copy(src, dst, refs[8].at[i])
        for i, (src, dst) in enumerate(zip(refs[:4], refs[4:8]))
    ]
    for copy in copies:
        copy.start()
    for copy in copies:
        copy.wait()


def shards(counts, u_factor, u_accum, v_factor, v_accum):
    vmem = pltpu.VMEM
    results = (
        pl.pallas_call(
            kernel,
            out_shape=tuple(
                jax.ShapeDtypeStruct(like.shape, f32) for like in (u_factor, u_accum, v_factor, v_accum)
            ),
            in_specs=[pl.BlockSpec(memory_space=pl.ANY)] * 5,
            out_specs=(pl.BlockSpec(memory_space=vmem),) * 4,
            scratch_shapes=[
                vmem((TOK_DEV, TEN_DEV), jnp.int32),
                vmem((PAD, TEN_DEV), bf16),
                vmem((1, TEN_DEV), f32),
                vmem((1, TEN_DEV), f32),
                vmem((4, TOK_DEV), f32),
                vmem((4, TOK_DEV), f32),
                vmem((64, 128), f32),
                vmem((2, 128), f32),
                vmem((2, 128), f32),
                vmem((16, 64, 128), bf16),
                vmem((RANK, PAD), bf16),
                vmem((PAD, RANK), bf16),
                vmem((256, 256), bf16),
                vmem((64, 2, 128), f32),
                vmem((16, 2, 128), f32),
                vmem((4, 16, TEN_DEV), f32),
                vmem((4, 16, TEN_DEV), f32),
                vmem((16, 16, TEN_DEV), bf16),
                vmem((2, 16, TEN_DEV), f32),
                vmem((4, 16, TEN_DEV), bf16),
                vmem((CHUNKS, 16, 16, 128), bf16),
                vmem((CHUNKS, 16, 16, 128), bf16),
                vmem((16, 128), f32),
                vmem((4, PAD), f32),
                pltpu.SemaphoreType.DMA((4 + CHUNKS,)),
                pltpu.SemaphoreType.DMA((6 + CHUNKS,)),
                pltpu.SemaphoreType.DMA((6 + CHUNKS,)),
            ],
            compiler_params=pltpu.CompilerParams(
                collective_id=0, has_side_effects=True, vmem_limit_bytes=57 << 20
            ),
        )(counts.T, u_factor, u_accum, v_factor, v_accum)
    )
    return pl.pallas_call(
        store,
        out_shape=tuple(jax.ShapeDtypeStruct(like.shape, f32) for like in results),
        in_specs=[pl.BlockSpec(memory_space=vmem)] * 4,
        out_specs=(pl.BlockSpec(memory_space=pl.ANY),) * 4,
        scratch_shapes=[pltpu.SemaphoreType.DMA((4,))],
    )(*results)


def solution(mesh):
    return jax.shard_map(
        shards,
        mesh=mesh,
        in_specs=(
            P("ten", "tok"),
            P("tok", "ten"),
            P("tok", "ten"),
            P("ten", "tok"),
            P("ten", "tok"),
        ),
        out_specs=(P("tok", "ten"), P("tok", "ten"), P("ten", "tok"), P("ten", "tok")),
        check_vma=False,
    )
```

```python
import jax
import jax.numpy as jnp
from jax import lax
from jax.experimental import pallas as pl
from jax.experimental.pallas import tpu as pltpu
from jax.sharding import PartitionSpec as P

MESH = pl.DeviceIdType.MESH
step_rate = 0.3
RANK = 64
TEN_DEV = 256
TOK_DEV = 2004
PAD = 2048
CHUNK = 512
CHUNKS = PAD // CHUNK
f32, bf16 = jnp.float32, jnp.bfloat16


def place():
    tok, ten = lax.axis_index("tok"), lax.axis_index("ten")
    return tok // 32, (tok // 2) % 16, tok % 2, ten // 2, ten % 2


def tok_at(half, z, core):
    return {"tok": half * 32 + z * 2 + core}


def ten_at(y, x):
    return {"ten": y * 2 + x}


def far_first(step, size):
    return size // 2 + ((step + 1) // 2) * (1 - 2 * (step % 2))


def each_z(body):
    _, z, _, _, _ = place()

    def one(step, carry):
        body((z + far_first(step, 16)) % 16)
        return carry

    lax.fori_loop(0, 15, one, 0)


def each_quad(body):
    half, _, core, _, _ = place()
    for dh, dc in ((1, 1), (1, 0), (0, 1)):
        body((half + dh) % 2, (core + dc) % 2)


def each_core(step, body):
    half, z, core, _, _ = place()
    peer_z = (z + far_first(step, 16)) % 16
    for dh, dc in ((1, 1), (1, 0), (0, 1), (0, 0)):
        body((half + dh) % 2, peer_z, (core + dc) % 2)


def each_x(step, body):
    _, _, _, y, x = place()
    peer_y = (y + far_first(step, 8)) % 8
    for dx in (1, 0):
        body(peer_y, (x + dx) % 2)


def each_tok(body):
    _, z, _, _, _ = place()

    def one(step, carry):
        each_core(step, body)
        return carry

    lax.fori_loop(0, 15, one, 0)
    each_quad(lambda h, c: body(h, z, c))


def each_ten(body):
    _, _, _, y, x = place()

    def one(step, carry):
        each_x(step, body)
        return carry

    lax.fori_loop(0, 7, one, 0)
    body(y, (x + 1) % 2)


def each_y(body):
    _, _, _, y, _ = place()

    def one(step, carry):
        body((y + far_first(step, 8)) % 8)
        return carry

    lax.fori_loop(0, 7, one, 0)


def send(src, dst, sems, phase, peer):
    send_sem, recv_sem = sems
    pltpu.make_async_remote_copy(
        src_ref=src,
        dst_ref=dst,
        send_sem=send_sem.at[phase],
        recv_sem=recv_sem.at[phase],
        device_id=peer,
        device_id_type=MESH,
    ).start()


def wait_bytes(like, sem):
    pltpu.make_async_copy(like, like, sem).wait()


def kernel(
    counts, u_factor, u_accum, v_factor, v_accum,
    u_next, u_accum_next, v_next, v_accum_next,
    cnt, weight, u_in, ua_in, v_in, va_in, v_rows, u_row, ua_row,
    v_all, v_ranks, v_half, order, u_all, ua_all,
    gu_out, gu_in, gu_z, u_rows, fresh, gv_out, gv_in, gv_x, gv_mid, gv_y, gv_sum, g_tile,
    local_sem, send_sem, recv_sem,
):
    half, z, core, y, x = place()
    ten = x * 8 + y
    quad = half * 2 + core
    slot = quad * 16 + z
    sems = (send_sem, recv_sem)

    loads = [
        pltpu.make_async_copy(src, dst, local_sem.at[i])
        for i, (src, dst) in enumerate(
            ((v_factor, v_in), (u_factor, u_in), (u_accum, ua_in), (v_accum, va_in))
        )
    ]
    for q in range(CHUNKS):
        rows = pl.ds(q * CHUNK, min(CHUNK, TOK_DEV - q * CHUNK))
        loads.append(pltpu.make_async_copy(counts.at[rows], cnt.at[rows], local_sem.at[4 + q]))
    for load in loads:
        load.start()

    barrier = pltpu.get_barrier_semaphore()

    def greet(peer):
        pl.semaphore_signal(barrier, inc=1, device_id=peer, device_id_type=MESH)

    each_tok(lambda h, pz, c: greet(tok_at(h, pz, c)))
    each_ten(lambda py, px: greet(ten_at(py, px)))

    v_rows[60:64, :] = jnp.zeros((4, 128), f32)
    loads[0].wait()
    for b in range(16):
        width = min(128, TOK_DEV - b * 128)
        v_rows[4 * b : 4 * b + 4, :width] = v_in[:, b * 128 : b * 128 + width]
    v_all[ten] = v_rows[...].astype(bf16)
    loads[1].wait()
    loads[2].wait()
    for b in range(2):
        u_row[b : b + 1, :] = u_in[:, b * 128 : b * 128 + 128]
        ua_row[b : b + 1, :] = ua_in[:, b * 128 : b * 128 + 128]
    u_all[slot] = u_row[...]
    ua_all[z] = ua_row[...]

    pl.semaphore_wait(barrier, 78)

    def send_u(h, pz, c):
        send(u_row, u_all.at[slot], sems, 0, tok_at(h, pz, c))

    def send_v(py, px):
        send(v_all.at[ten], v_all.at[ten], sems, 2, ten_at(py, px))

    def send_both(step, carry):
        each_core(step, send_u)
        each_x(step, send_v)
        return carry

    def send_rest(step, carry):
        each_core(step, send_u)
        return carry

    lax.fori_loop(0, 7, send_both, 0)
    send_v(y, (x + 1) % 2)
    lax.fori_loop(7, 15, send_rest, 0)
    each_quad(lambda h, c: send_u(h, z, c))
    each_z(lambda pz: send(ua_row, ua_all.at[z], sems, 1, tok_at(half, pz, core)))

    row = lax.broadcasted_iota(jnp.int32, (256, 256), 0)
    col = lax.broadcasted_iota(jnp.int32, (256, 256), 1)
    rank = ((row >> 4) & 7) * 8 + (row >> 7) * 4 + (row & 3)
    col_rank = (col & 32) + (col & 15) * 2 + ((col >> 4) & 1)
    same = (((row >> 2) & 3) == (col >> 6)) & (rank == col_rank)
    order[...] = jnp.where(same, 1.0, 0.0).astype(bf16)

    weight[PAD - 48 :, :] = jnp.zeros((48, TEN_DEV), bf16)
    for q in range(CHUNKS):
        loads[4 + q].wait()
        rows = slice(q * CHUNK, min(q * CHUNK + CHUNK, TOK_DEV))
        weight[rows, :] = (0.5 + 0.25 * cnt[rows, :].astype(f32)).astype(bf16)

    wait_bytes(v_all.at[pl.ds(0, 15)], recv_sem.at[2])
    for q in range(CHUNKS):
        block = v_all[:, 16 * q : 16 * q + 16, :].reshape(256, 128)
        ranks = lax.dot_general(
            order[...], block, (((0,), (0,)), ((), ())), preferred_element_type=f32
        )
        for b in range(4):
            start = q * CHUNK + b * 128
            v_ranks[:, start : start + 128] = ranks[64 * b : 64 * b + 64, :].astype(bf16)
            v_half[start : start + 128, :] = (0.5 * ranks[64 * b : 64 * b + 64, :]).T.astype(bf16)

    def residual(low, q):
        rows = slice(q * CHUNK, (q + 1) * CHUNK)
        t = jnp.tanh(jnp.dot(v_half[rows, :], low, preferred_element_type=f32))
        return (weight[rows, :].astype(f32) * (1.0 - t) - 1.0).astype(bf16)

    wait_bytes(u_all.at[pl.ds(0, 63)], recv_sem.at[0])
    u_full = jnp.concatenate([u_all[:, 0, :], u_all[:, 1, :]], axis=1)
    low = u_full.astype(bf16)
    grad_u = jnp.zeros((RANK, TEN_DEV), f32)
    for q in range(CHUNKS):
        grad_u += jnp.dot(
            v_ranks[:, q * CHUNK : (q + 1) * CHUNK], residual(low, q), preferred_element_type=f32
        )
    gu_out[...] = grad_u.reshape(4, 16, TEN_DEV)

    each_quad(lambda h, c: send(gu_out.at[h * 2 + c], gu_in.at[quad], sems, 3, tok_at(h, z, c)))
    gu_in[quad] = gu_out[quad]
    wait_bytes(gu_in.at[pl.ds(0, 3)], recv_sem.at[3])
    gu_z[z] = ((gu_in[0] + gu_in[1]) + (gu_in[2] + gu_in[3])).astype(bf16)
    each_z(lambda pz: send(gu_z.at[z], gu_z.at[z], sems, 4, tok_at(half, pz, core)))
    wait_bytes(ua_all.at[pl.ds(0, 15)], recv_sem.at[1])
    mine = u_all[pl.ds(quad * 16, 16)]
    factor = jnp.concatenate([mine[:, 0, :], mine[:, 1, :]], axis=1)
    accum = jnp.concatenate([ua_all[:, 0, :], ua_all[:, 1, :]], axis=1)
    wait_bytes(gu_z.at[pl.ds(0, 15)], recv_sem.at[4])
    grad = jnp.sum(gu_z[...].astype(f32), axis=0)
    accum = accum + grad * grad
    factor = factor + step_rate * grad / jnp.sqrt(accum)
    fresh[quad] = factor.astype(bf16)
    each_quad(lambda h, c: send(fresh.at[quad], fresh.at[quad], sems, 5, tok_at(h, z, c)))
    u_rows[0] = factor
    u_rows[1] = accum
    u_next[...] = u_rows[0, pl.ds(z, 1), :]
    u_accum_next[...] = u_rows[1, pl.ds(z, 1), :]
    wait_bytes(fresh.at[pl.ds(0, 3)], recv_sem.at[5])

    low = fresh[...].reshape(RANK, TEN_DEV)
    for q in range(CHUNKS):
        part = lax.dot_general(
            low, residual(low, q), (((1,), (1,)), ((), ())), preferred_element_type=f32
        ).astype(bf16)
        stacked = jnp.concatenate([part[:, 128 * b : 128 * b + 128] for b in range(4)], axis=0)
        pieces = jnp.dot(order[...], stacked, preferred_element_type=f32).astype(bf16)
        gv_out[q] = pieces.reshape(16, 16, 128)
        if q % 2 == 0:
            other = gv_out.at[q, pl.ds((1 - x) * 8, 8)]
            send(other, gv_x.at[q // 2], sems, 6 + q, ten_at(y, 1 - x))
        else:
            each_ten(lambda py, px: send(gv_out.at[q, px * 8 + py], gv_in.at[q // 2, ten], sems, 6 + q, ten_at(py, px)))
            gv_in[q // 2, ten] = gv_out[q, ten]
    for q in range(0, CHUNKS, 2):
        i = q // 2
        wait_bytes(gv_x.at[i], recv_sem.at[6 + q])
        pair = gv_out[q, pl.ds(x * 8, 8)].astype(f32) + gv_x[i].astype(f32)
        gv_mid[i] = pair.astype(bf16)
        each_y(lambda py: send(gv_mid.at[i, py], gv_y.at[i, y], sems, 6 + CHUNKS + i, ten_at(py, x)))
        gv_y[i, y] = gv_mid[i, y]

    loads[3].wait()
    for q in (1, 3, 0, 2):
        i = q // 2
        if q % 2 == 0:
            wait_bytes(gv_y.at[i, pl.ds(0, 7)], recv_sem.at[6 + CHUNKS + i])
            gv_sum[...] = jnp.sum(gv_y[i].astype(f32), axis=0)
        else:
            wait_bytes(gv_in.at[i, pl.ds(0, 15)], recv_sem.at[6 + q])
            gv_sum[...] = jnp.sum(gv_in[i].astype(f32), axis=0)
        for b in range(4):
            start = q * CHUNK + b * 128
            g_tile[:, start : start + 128] = gv_sum[4 * b : 4 * b + 4, :]
    grad = g_tile[:, :TOK_DEV]
    accum = va_in[...] + grad * grad
    v_accum_next[...] = accum
    v_next[...] = v_in[...] + step_rate * grad / jnp.sqrt(accum)

    wait_bytes(u_all.at[pl.ds(0, 63)], send_sem.at[0])
    wait_bytes(ua_all.at[pl.ds(0, 15)], send_sem.at[1])
    wait_bytes(v_all.at[pl.ds(0, 15)], send_sem.at[2])
    wait_bytes(gu_in.at[pl.ds(0, 3)], send_sem.at[3])
    wait_bytes(gu_z.at[pl.ds(0, 15)], send_sem.at[4])
    wait_bytes(fresh.at[pl.ds(0, 3)], send_sem.at[5])
    for i in range(CHUNKS // 2):
        wait_bytes(gv_x.at[i], send_sem.at[6 + 2 * i])
        wait_bytes(gv_in.at[i, pl.ds(0, 15)], send_sem.at[7 + 2 * i])
        wait_bytes(gv_y.at[i, pl.ds(0, 7)], send_sem.at[6 + CHUNKS + i])


def store(*refs):
    copies = [
        pltpu.make_async_copy(src, dst, refs[8].at[i])
        for i, (src, dst) in enumerate(zip(refs[:4], refs[4:8]))
    ]
    for copy in copies:
        copy.start()
    for copy in copies:
        copy.wait()


def shards(counts, u_factor, u_accum, v_factor, v_accum):
    vmem = pltpu.VMEM
    results = (
        pl.pallas_call(
            kernel,
            out_shape=tuple(
                jax.ShapeDtypeStruct(like.shape, f32) for like in (u_factor, u_accum, v_factor, v_accum)
            ),
            in_specs=[pl.BlockSpec(memory_space=pl.ANY)] * 5,
            out_specs=(pl.BlockSpec(memory_space=vmem),) * 4,
            scratch_shapes=[
                vmem((TOK_DEV, TEN_DEV), jnp.int32),
                vmem((PAD, TEN_DEV), bf16),
                vmem((1, TEN_DEV), f32),
                vmem((1, TEN_DEV), f32),
                vmem((4, TOK_DEV), f32),
                vmem((4, TOK_DEV), f32),
                vmem((64, 128), f32),
                vmem((2, 128), f32),
                vmem((2, 128), f32),
                vmem((16, 64, 128), bf16),
                vmem((RANK, PAD), bf16),
                vmem((PAD, RANK), bf16),
                vmem((256, 256), bf16),
                vmem((64, 2, 128), f32),
                vmem((16, 2, 128), f32),
                vmem((4, 16, TEN_DEV), f32),
                vmem((4, 16, TEN_DEV), f32),
                vmem((16, 16, TEN_DEV), bf16),
                vmem((2, 16, TEN_DEV), f32),
                vmem((4, 16, TEN_DEV), bf16),
                vmem((CHUNKS, 16, 16, 128), bf16),
                vmem((CHUNKS // 2, 16, 16, 128), bf16),
                vmem((CHUNKS // 2, 8, 16, 128), bf16),
                vmem((CHUNKS // 2, 8, 16, 128), bf16),
                vmem((CHUNKS // 2, 8, 16, 128), bf16),
                vmem((16, 128), f32),
                vmem((4, PAD), f32),
                pltpu.SemaphoreType.DMA((4 + CHUNKS,)),
                pltpu.SemaphoreType.DMA((6 + CHUNKS + CHUNKS // 2,)),
                pltpu.SemaphoreType.DMA((6 + CHUNKS + CHUNKS // 2,)),
            ],
            compiler_params=pltpu.CompilerParams(
                collective_id=0, has_side_effects=True, vmem_limit_bytes=40 << 20
            ),
        )(*(pltpu.with_memory_space_constraint(a, pltpu.HBM) for a in (counts.T, u_factor, u_accum, v_factor, v_accum)))
    )
    return pl.pallas_call(
        store,
        out_shape=tuple(jax.ShapeDtypeStruct(like.shape, f32) for like in results),
        in_specs=[pl.BlockSpec(memory_space=vmem)] * 4,
        out_specs=(pl.BlockSpec(memory_space=pl.ANY),) * 4,
        scratch_shapes=[pltpu.SemaphoreType.DMA((4,))],
        compiler_params=pltpu.CompilerParams(vmem_limit_bytes=1 << 20),
    )(*results)


def solution(mesh):
    return jax.shard_map(
        shards,
        mesh=mesh,
        in_specs=(
            P("ten", "tok"),
            P("tok", "ten"),
            P("tok", "ten"),
            P("ten", "tok"),
            P("ten", "tok"),
        ),
        out_specs=(P("tok", "ten"), P("tok", "ten"), P("ten", "tok"), P("ten", "tok")),
        check_vma=False,
    )
```

```python
import jax
import jax.numpy as jnp
from jax import lax
from jax.experimental import pallas as pl
from jax.experimental.pallas import tpu as pltpu
from jax.sharding import PartitionSpec as P

MESH = pl.DeviceIdType.MESH
step_rate = 0.3
RANK = 64
TEN_DEV = 256
TOK_DEV = 2004
PAD = 2048
CHUNK = 512
CHUNKS = PAD // CHUNK
PAIRED = (0, 1)
STRAIGHT = tuple(q for q in range(CHUNKS) if q not in PAIRED)
f32, bf16 = jnp.float32, jnp.bfloat16


def place():
    tok, ten = lax.axis_index("tok"), lax.axis_index("ten")
    return tok // 32, (tok // 2) % 16, tok % 2, ten // 2, ten % 2


def tok_at(half, z, core):
    return {"tok": half * 32 + z * 2 + core}


def ten_at(y, x):
    return {"ten": y * 2 + x}


def far_first(step, size):
    return size // 2 + ((step + 1) // 2) * (1 - 2 * (step % 2))


def each_z(body):
    _, z, _, _, _ = place()

    def one(step, carry):
        body((z + far_first(step, 16)) % 16)
        return carry

    lax.fori_loop(0, 15, one, 0)


def each_quad(body):
    half, _, core, _, _ = place()
    for dh, dc in ((1, 1), (1, 0), (0, 1)):
        body((half + dh) % 2, (core + dc) % 2)


def each_core(step, body):
    half, z, core, _, _ = place()
    peer_z = (z + far_first(step, 16)) % 16
    for dh, dc in ((1, 1), (1, 0), (0, 1), (0, 0)):
        body((half + dh) % 2, peer_z, (core + dc) % 2)


def each_x(step, body):
    _, _, _, y, x = place()
    peer_y = (y + far_first(step, 8)) % 8
    for dx in (1, 0):
        body(peer_y, (x + dx) % 2)


def each_tok(body):
    _, z, _, _, _ = place()

    def one(step, carry):
        each_core(step, body)
        return carry

    lax.fori_loop(0, 15, one, 0, unroll=5)
    each_quad(lambda h, c: body(h, z, c))


def each_ten(body):
    _, _, _, y, x = place()

    def one(step, carry):
        each_x(step, body)
        return carry

    lax.fori_loop(0, 7, one, 0, unroll=7)
    body(y, (x + 1) % 2)


def each_y(body):
    _, _, _, y, _ = place()

    def one(step, carry):
        body((y + far_first(step, 8)) % 8)
        return carry

    lax.fori_loop(0, 7, one, 0)


def send(src, dst, sems, phase, peer):
    send_sem, recv_sem = sems
    pltpu.make_async_remote_copy(
        src_ref=src,
        dst_ref=dst,
        send_sem=send_sem.at[phase],
        recv_sem=recv_sem.at[phase],
        device_id=peer,
        device_id_type=MESH,
    ).start()


def wait_bytes(like, sem):
    pltpu.make_async_copy(like, like, sem).wait()


def kernel(
    counts, u_factor, u_accum, v_factor, v_accum,
    u_next, u_accum_next, v_next, v_accum_next,
    cnt, weight, u_in, ua_in, v_in, va_in, v_rows, u_row, ua_row,
    v_all, v_ranks, v_half, order, u_all, ua_all,
    gu_out, gu_in, gu_z, u_rows, u_pair, u_got, fresh, gv_out, gv_in, gv_x, gv_mid, gv_y, gv_sum, g_tile,
    local_sem, send_sem, recv_sem,
):
    half, z, core, y, x = place()
    ten = x * 8 + y
    slot = half * 32 + core * 16 + z
    sems = (send_sem, recv_sem)

    loads = [
        pltpu.make_async_copy(src, dst, local_sem.at[i])
        for i, (src, dst) in enumerate(
            ((v_factor, v_in), (u_factor, u_in), (u_accum, ua_in), (v_accum, va_in))
        )
    ]
    for q in range(CHUNKS):
        rows = pl.ds(q * CHUNK, min(CHUNK, TOK_DEV - q * CHUNK))
        loads.append(pltpu.make_async_copy(counts.at[rows], cnt.at[rows], local_sem.at[4 + q]))
    for load in loads:
        load.start()

    barrier = pltpu.get_barrier_semaphore()

    def greet(peer):
        pl.semaphore_signal(barrier, inc=1, device_id=peer, device_id_type=MESH)

    each_tok(lambda h, pz, c: greet(tok_at(h, pz, c)))
    each_ten(lambda py, px: greet(ten_at(py, px)))

    v_rows[60:64, :] = jnp.zeros((4, 128), f32)
    loads[0].wait()
    for b in range(16):
        width = min(128, TOK_DEV - b * 128)
        v_rows[4 * b : 4 * b + 4, :width] = v_in[:, b * 128 : b * 128 + width]
    v_all[ten] = v_rows[...].astype(bf16)
    loads[1].wait()
    loads[2].wait()
    for b in range(2):
        u_row[b : b + 1, :] = u_in[:, b * 128 : b * 128 + 128]
        ua_row[b : b + 1, :] = ua_in[:, b * 128 : b * 128 + 128]
    u_all[slot] = u_row[...]

    @pl.when(core == 1)
    def _():
        ua_all[16 + z] = ua_row[...]

    pl.semaphore_wait(barrier, 78)

    def send_u(h, pz, c):
        send(u_row, u_all.at[slot], sems, 0, tok_at(h, pz, c))

    def send_v(py, px):
        send(v_all.at[ten], v_all.at[ten], sems, 2, ten_at(py, px))

    def send_both(step, carry):
        each_core(step, send_u)
        each_x(step, send_v)
        return carry

    def send_rest(step, carry):
        each_core(step, send_u)
        return carry

    lax.fori_loop(0, 7, send_both, 0)
    send_v(y, (x + 1) % 2)
    lax.fori_loop(7, 15, send_rest, 0)
    each_quad(lambda h, c: send_u(h, z, c))
    each_z(lambda pz: send(ua_row, ua_all.at[core * 16 + z], sems, 1, tok_at(half, pz, 1)))

    @pl.when(core == 0)
    def _():
        send(ua_row, ua_all.at[z], sems, 1, tok_at(half, z, 1))


    row = lax.broadcasted_iota(jnp.int32, (256, 256), 0)
    col = lax.broadcasted_iota(jnp.int32, (256, 256), 1)
    rank = ((row >> 4) & 7) * 8 + (row >> 7) * 4 + (row & 3)
    col_rank = (col & 32) + (col & 15) * 2 + ((col >> 4) & 1)
    same = (((row >> 2) & 3) == (col >> 6)) & (rank == col_rank)
    order[...] = jnp.where(same, 1.0, 0.0).astype(bf16)

    weight[PAD - 48 :, :] = jnp.zeros((48, TEN_DEV), bf16)
    for q in range(CHUNKS):
        loads[4 + q].wait()
        rows = slice(q * CHUNK, min(q * CHUNK + CHUNK, TOK_DEV))
        weight[rows, :] = (0.5 + 0.25 * cnt[rows, :].astype(f32)).astype(bf16)

    wait_bytes(v_all.at[pl.ds(0, 15)], recv_sem.at[2])
    for q in range(CHUNKS):
        block = v_all[:, 16 * q : 16 * q + 16, :].reshape(256, 128)
        ranks = lax.dot_general(
            order[...], block, (((0,), (0,)), ((), ())), preferred_element_type=f32
        )
        for b in range(4):
            start = q * CHUNK + b * 128
            v_ranks[:, start : start + 128] = ranks[64 * b : 64 * b + 64, :].astype(bf16)
            v_half[start : start + 128, :] = (0.5 * ranks[64 * b : 64 * b + 64, :]).T.astype(bf16)

    def residual(low, q):
        rows = slice(q * CHUNK, (q + 1) * CHUNK)
        t = jnp.tanh(jnp.dot(v_half[rows, :], low, preferred_element_type=f32))
        return (weight[rows, :].astype(f32) * (1.0 - t) - 1.0).astype(bf16)

    wait_bytes(u_all.at[pl.ds(0, 63)], recv_sem.at[0])
    u_full = jnp.concatenate([u_all[:, 0, :], u_all[:, 1, :]], axis=1)
    low = u_full.astype(bf16)
    grad_u = jnp.zeros((RANK, TEN_DEV), f32)
    for q in range(CHUNKS):
        grad_u += jnp.dot(
            v_ranks[:, q * CHUNK : (q + 1) * CHUNK], residual(low, q), preferred_element_type=f32
        )
    gu_out[...] = grad_u.reshape(2, 32, TEN_DEV).astype(bf16)

    send(gu_out.at[1 - half], gu_in.at[2 - core], sems, 3, tok_at(1 - half, z, 1))

    @pl.when(core == 0)
    def _():
        send(gu_out.at[half], gu_in.at[0], sems, 3, tok_at(half, z, 1))

    @pl.when(core == 1)
    def _():
        mine = u_all[pl.ds(half * 32, 32)]
        wait_bytes(ua_all.at[pl.ds(0, 31)], recv_sem.at[1])
        factor = jnp.concatenate([mine[:, 0, :], mine[:, 1, :]], axis=1)
        accum = jnp.concatenate([ua_all[:, 0, :], ua_all[:, 1, :]], axis=1)
        wait_bytes(gu_in, recv_sem.at[3])
        total = gu_out[half].astype(f32) + jnp.sum(gu_in[...].astype(f32), axis=0)
        gu_z[z] = total.astype(bf16)
        each_z(lambda pz: send(gu_z.at[z], gu_z.at[z], sems, 4, tok_at(half, pz, 1)))
        wait_bytes(gu_z.at[pl.ds(0, 15)], recv_sem.at[4])
        grad = jnp.sum(gu_z[...].astype(f32), axis=0)
        accum = accum + grad * grad
        factor = factor + step_rate * grad / jnp.sqrt(accum)
        fresh[half] = factor.astype(bf16)
        for h, c in ((1 - half, 0), (1 - half, 1), (half, 0)):
            send(fresh.at[half], fresh.at[half], sems, 5, tok_at(h, z, c))
        u_rows[0] = factor
        u_rows[1] = accum
        for i in range(2):
            u_pair[i : i + 1, :] = u_rows[i, pl.ds(z, 1), :]
        send(u_pair, u_got, sems, 6, tok_at(half, z, 0))
        u_next[...] = u_rows[0, pl.ds(16 + z, 1), :]
        u_accum_next[...] = u_rows[1, pl.ds(16 + z, 1), :]
        wait_bytes(fresh.at[0], recv_sem.at[5])

    @pl.when(core == 0)
    def _():
        wait_bytes(fresh, recv_sem.at[5])

    low = fresh[...].reshape(RANK, TEN_DEV)
    for q in range(CHUNKS):
        part = lax.dot_general(
            low, residual(low, q), (((1,), (1,)), ((), ())), preferred_element_type=f32
        ).astype(bf16)
        stacked = jnp.concatenate([part[:, 128 * b : 128 * b + 128] for b in range(4)], axis=0)
        pieces = jnp.dot(order[...], stacked, preferred_element_type=f32).astype(bf16)
        gv_out[q] = pieces.reshape(16, 16, 128)
        if q in PAIRED:
            other = gv_out.at[q, pl.ds((1 - x) * 8, 8)]
            send(other, gv_x.at[PAIRED.index(q)], sems, 7 + q, ten_at(y, 1 - x))
        else:
            i = STRAIGHT.index(q)
            each_ten(lambda py, px: send(gv_out.at[q, px * 8 + py], gv_in.at[i, ten], sems, 7 + q, ten_at(py, px)))
            gv_in[i, ten] = gv_out[q, ten]
    for i, q in enumerate(PAIRED):
        wait_bytes(gv_x.at[i], recv_sem.at[7 + q])
        pair = gv_out[q, pl.ds(x * 8, 8)].astype(f32) + gv_x[i].astype(f32)
        gv_mid[i] = pair.astype(bf16)
        each_y(lambda py: send(gv_mid.at[i, py], gv_y.at[i, y], sems, 7 + CHUNKS + i, ten_at(py, x)))
        gv_y[i, y] = gv_mid[i, y]

    loads[3].wait()
    for q in STRAIGHT + PAIRED:
        if q in PAIRED:
            i = PAIRED.index(q)
            wait_bytes(gv_y.at[i, pl.ds(0, 7)], recv_sem.at[7 + CHUNKS + i])
            gv_sum[...] = jnp.sum(gv_y[i].astype(f32), axis=0)
        else:
            i = STRAIGHT.index(q)
            wait_bytes(gv_in.at[i, pl.ds(0, 15)], recv_sem.at[7 + q])
            gv_sum[...] = jnp.sum(gv_in[i].astype(f32), axis=0)
        for b in range(4):
            start = q * CHUNK + b * 128
            g_tile[:, start : start + 128] = gv_sum[4 * b : 4 * b + 4, :]
        cols = slice(q * CHUNK, min(q * CHUNK + CHUNK, TOK_DEV))
        grad = g_tile[:, cols]
        accum = va_in[:, cols] + grad * grad
        v_accum_next[:, cols] = accum
        v_next[:, cols] = v_in[:, cols] + step_rate * grad / jnp.sqrt(accum)

    wait_bytes(u_all.at[pl.ds(0, 63)], send_sem.at[0])
    wait_bytes(ua_all.at[pl.ds(0, 15)], send_sem.at[1])
    wait_bytes(v_all.at[pl.ds(0, 15)], send_sem.at[2])
    wait_bytes(gu_out.at[0], send_sem.at[3])

    @pl.when(core == 0)
    def _():
        wait_bytes(ua_row, send_sem.at[1])
        wait_bytes(gu_out.at[0], send_sem.at[3])
        wait_bytes(u_got, recv_sem.at[6])
        u_next[...] = u_got[0:1, :]
        u_accum_next[...] = u_got[1:2, :]

    @pl.when(core == 1)
    def _():
        wait_bytes(gu_z.at[pl.ds(0, 15)], send_sem.at[4])
        wait_bytes(gu_in, send_sem.at[5])
        wait_bytes(u_pair, send_sem.at[6])

    for i, q in enumerate(PAIRED):
        wait_bytes(gv_x.at[i], send_sem.at[7 + q])
        wait_bytes(gv_y.at[i, pl.ds(0, 7)], send_sem.at[7 + CHUNKS + i])
    for i, q in enumerate(STRAIGHT):
        wait_bytes(gv_in.at[i, pl.ds(0, 15)], send_sem.at[7 + q])


def store(*refs):
    copies = [
        pltpu.make_async_copy(src, dst, refs[8].at[i])
        for i, (src, dst) in enumerate(zip(refs[:4], refs[4:8]))
    ]
    for copy in copies:
        copy.start()
    for copy in copies:
        copy.wait()


def shards(counts, u_factor, u_accum, v_factor, v_accum):
    vmem = pltpu.VMEM
    results = (
        pl.pallas_call(
            kernel,
            out_shape=tuple(
                jax.ShapeDtypeStruct(like.shape, f32) for like in (u_factor, u_accum, v_factor, v_accum)
            ),
            in_specs=[pl.BlockSpec(memory_space=pl.ANY)] * 5,
            out_specs=(pl.BlockSpec(memory_space=vmem),) * 4,
            scratch_shapes=[
                vmem((TOK_DEV, TEN_DEV), jnp.int32),
                vmem((PAD, TEN_DEV), bf16),
                vmem((1, TEN_DEV), f32),
                vmem((1, TEN_DEV), f32),
                vmem((4, TOK_DEV), f32),
                vmem((4, TOK_DEV), f32),
                vmem((64, 128), f32),
                vmem((2, 128), f32),
                vmem((2, 128), f32),
                vmem((16, 64, 128), bf16),
                vmem((RANK, PAD), bf16),
                vmem((PAD, RANK), bf16),
                vmem((256, 256), bf16),
                vmem((64, 2, 128), f32),
                vmem((32, 2, 128), f32),
                vmem((2, 32, TEN_DEV), bf16),
                vmem((3, 32, TEN_DEV), bf16),
                vmem((16, 32, TEN_DEV), bf16),
                vmem((2, 32, TEN_DEV), f32),
                vmem((2, TEN_DEV), f32),
                vmem((2, TEN_DEV), f32),
                vmem((2, 32, TEN_DEV), bf16),
                vmem((CHUNKS, 16, 16, 128), bf16),
                vmem((len(STRAIGHT), 16, 16, 128), bf16),
                vmem((len(PAIRED), 8, 16, 128), bf16),
                vmem((len(PAIRED), 8, 16, 128), bf16),
                vmem((len(PAIRED), 8, 16, 128), bf16),
                vmem((16, 128), f32),
                vmem((4, PAD), f32),
                pltpu.SemaphoreType.DMA((4 + CHUNKS,)),
                pltpu.SemaphoreType.DMA((7 + CHUNKS + len(PAIRED),)),
                pltpu.SemaphoreType.DMA((7 + CHUNKS + len(PAIRED),)),
            ],
            compiler_params=pltpu.CompilerParams(
                collective_id=0, has_side_effects=True, vmem_limit_bytes=40 << 20
            ),
        )(*(pltpu.with_memory_space_constraint(a, pltpu.HBM) for a in (counts.T, u_factor, u_accum, v_factor, v_accum)))
    )
    return pl.pallas_call(
        store,
        out_shape=tuple(jax.ShapeDtypeStruct(like.shape, f32) for like in results),
        in_specs=[pl.BlockSpec(memory_space=vmem)] * 4,
        out_specs=(pl.BlockSpec(memory_space=pl.ANY),) * 4,
        scratch_shapes=[pltpu.SemaphoreType.DMA((4,))],
        compiler_params=pltpu.CompilerParams(vmem_limit_bytes=1 << 20),
    )(*results)


def solution(mesh):
    return jax.shard_map(
        shards,
        mesh=mesh,
        in_specs=(
            P("ten", "tok"),
            P("tok", "ten"),
            P("tok", "ten"),
            P("ten", "tok"),
            P("ten", "tok"),
        ),
        out_specs=(P("tok", "ten"), P("tok", "ten"), P("ten", "tok"), P("ten", "tok")),
        check_vma=False,
    )
```

```python
import jax
import jax.numpy as jnp
from jax import lax
from jax.experimental import pallas as pl
from jax.experimental.pallas import tpu as pltpu
from jax.sharding import PartitionSpec as P

MESH = pl.DeviceIdType.MESH
step_rate = 0.3
RANK = 64
TEN_DEV = 256
TOK_DEV = 2004
PAD = 2048
CHUNK = 512
CHUNKS = PAD // CHUNK
PAIRED = (0,)
STRAIGHT = tuple(q for q in range(CHUNKS) if q not in PAIRED)
f32, bf16 = jnp.float32, jnp.bfloat16


def place():
    tok, ten = lax.axis_index("tok"), lax.axis_index("ten")
    return tok // 32, (tok // 2) % 16, tok % 2, ten // 2, ten % 2


def tok_at(half, z, core):
    return {"tok": half * 32 + z * 2 + core}


def ten_at(y, x):
    return {"ten": y * 2 + x}


def far_first(step, size):
    return size // 2 + ((step + 1) // 2) * (1 - 2 * (step % 2))


def each_z(body):
    _, z, _, _, _ = place()

    def one(step, carry):
        body((z + far_first(step, 16)) % 16)
        return carry

    lax.fori_loop(0, 15, one, 0)


def each_quad(body):
    half, _, core, _, _ = place()
    for dh, dc in ((1, 1), (1, 0), (0, 1)):
        body((half + dh) % 2, (core + dc) % 2)


def each_core(step, body):
    half, z, core, _, _ = place()
    peer_z = (z + far_first(step, 16)) % 16
    for dh, dc in ((1, 1), (1, 0), (0, 1), (0, 0)):
        body((half + dh) % 2, peer_z, (core + dc) % 2)


def each_x(step, body):
    _, _, _, y, x = place()
    peer_y = (y + far_first(step, 8)) % 8
    for dx in (1, 0):
        body(peer_y, (x + dx) % 2)


def each_tok(body):
    _, z, _, _, _ = place()

    def one(step, carry):
        each_core(step, body)
        return carry

    lax.fori_loop(0, 15, one, 0, unroll=5)
    each_quad(lambda h, c: body(h, z, c))


def each_ten(body):
    _, _, _, y, x = place()

    def one(step, carry):
        each_x(step, body)
        return carry

    lax.fori_loop(0, 7, one, 0, unroll=7)
    body(y, (x + 1) % 2)


def each_y(body):
    _, _, _, y, _ = place()

    def one(step, carry):
        body((y + far_first(step, 8)) % 8)
        return carry

    lax.fori_loop(0, 7, one, 0)


def send(src, dst, sems, phase, peer):
    send_sem, recv_sem = sems
    pltpu.make_async_remote_copy(
        src_ref=src,
        dst_ref=dst,
        send_sem=send_sem.at[phase],
        recv_sem=recv_sem.at[phase],
        device_id=peer,
        device_id_type=MESH,
    ).start()


def wait_bytes(like, sem):
    pltpu.make_async_copy(like, like, sem).wait()


def kernel(
    counts, u_factor, u_accum, v_factor, v_accum,
    u_next, u_accum_next, v_next, v_accum_next,
    cnt, weight, u_in, ua_in, v_in, va_in, v_rows, u_row, ua_row,
    v_all, v_ranks, v_half, order, u_all, ua_all,
    gu_out, gu_in, gu_z, u_rows, u_pair, u_got, fresh, framed, spread, gv_out, gv_in, gv_x, gv_mid, gv_y, gv_sum, g_tile,
    local_sem, send_sem, recv_sem,
):
    half, z, core, y, x = place()
    ten = x * 8 + y
    slot = half * 32 + core * 16 + z
    sems = (send_sem, recv_sem)

    loads = [
        pltpu.make_async_copy(src, dst, local_sem.at[i])
        for i, (src, dst) in enumerate(
            ((v_factor, v_in), (u_factor, u_in), (u_accum, ua_in), (v_accum, va_in))
        )
    ]
    for q in range(CHUNKS):
        rows = pl.ds(q * CHUNK, min(CHUNK, TOK_DEV - q * CHUNK))
        loads.append(pltpu.make_async_copy(counts.at[rows], cnt.at[rows], local_sem.at[4 + q]))
    for load in loads:
        load.start()

    barrier = pltpu.get_barrier_semaphore()

    def greet(peer):
        pl.semaphore_signal(barrier, inc=1, device_id=peer, device_id_type=MESH)

    each_tok(lambda h, pz, c: greet(tok_at(h, pz, c)))
    each_ten(lambda py, px: greet(ten_at(py, px)))

    v_rows[60:64, :] = jnp.zeros((4, 128), f32)
    loads[0].wait()
    for b in range(16):
        width = min(128, TOK_DEV - b * 128)
        v_rows[4 * b : 4 * b + 4, :width] = v_in[:, b * 128 : b * 128 + width]
    v_all[ten] = v_rows[...].astype(bf16)
    loads[1].wait()
    loads[2].wait()
    for b in range(2):
        u_row[b : b + 1, :] = u_in[:, b * 128 : b * 128 + 128]
        ua_row[b : b + 1, :] = ua_in[:, b * 128 : b * 128 + 128]
    u_all[slot] = u_row[...]

    @pl.when(core == 1)
    def _():
        ua_all[16 + z] = ua_row[...]

    pl.semaphore_wait(barrier, 78)

    def send_u(h, pz, c):
        send(u_row, u_all.at[slot], sems, 0, tok_at(h, pz, c))

    def send_v(py, px):
        send(v_all.at[ten], v_all.at[ten], sems, 2, ten_at(py, px))

    def send_both(step, carry):
        each_core(step, send_u)
        each_x(step, send_v)
        return carry

    def send_rest(step, carry):
        each_core(step, send_u)
        return carry

    lax.fori_loop(0, 7, send_both, 0)
    send_v(y, (x + 1) % 2)
    lax.fori_loop(7, 15, send_rest, 0)
    each_quad(lambda h, c: send_u(h, z, c))
    each_z(lambda pz: send(ua_row, ua_all.at[core * 16 + z], sems, 1, tok_at(half, pz, 1)))

    @pl.when(core == 0)
    def _():
        send(ua_row, ua_all.at[z], sems, 1, tok_at(half, z, 1))


    row = lax.broadcasted_iota(jnp.int32, (256, 256), 0)
    col = lax.broadcasted_iota(jnp.int32, (256, 256), 1)
    rank = ((row >> 4) & 7) * 8 + (row >> 7) * 4 + (row & 3)
    col_rank = (col & 32) + (col & 15) * 2 + ((col >> 4) & 1)
    same = (((row >> 2) & 3) == (col >> 6)) & (rank == col_rank)
    order[...] = jnp.where(same, 1.0, 0.0).astype(bf16)

    framed[...] = jnp.zeros((448, TEN_DEV), bf16)

    weight[PAD - 48 :, :] = jnp.zeros((48, TEN_DEV), bf16)
    for q in range(CHUNKS):
        loads[4 + q].wait()
        rows = slice(q * CHUNK, min(q * CHUNK + CHUNK, TOK_DEV))
        weight[rows, :] = (0.5 + 0.25 * cnt[rows, :].astype(f32)).astype(bf16)

    wait_bytes(v_all.at[pl.ds(0, 15)], recv_sem.at[2])
    for q in range(CHUNKS):
        block = v_all[:, 16 * q : 16 * q + 16, :].reshape(256, 128)
        ranks = lax.dot_general(
            order[...], block, (((0,), (0,)), ((), ())), preferred_element_type=f32
        )
        for b in range(4):
            start = q * CHUNK + b * 128
            v_ranks[:, start : start + 128] = ranks[64 * b : 64 * b + 64, :].astype(bf16)
            v_half[start : start + 128, :] = (0.5 * ranks[64 * b : 64 * b + 64, :]).T.astype(bf16)

    def residual(low, q):
        rows = slice(q * CHUNK, (q + 1) * CHUNK)
        t = jnp.tanh(jnp.dot(v_half[rows, :], low, preferred_element_type=f32))
        return (weight[rows, :].astype(f32) * (1.0 - t) - 1.0).astype(bf16)

    wait_bytes(u_all.at[pl.ds(0, 63)], recv_sem.at[0])
    u_full = jnp.concatenate([u_all[:, 0, :], u_all[:, 1, :]], axis=1)
    low = u_full.astype(bf16)
    grad_u = jnp.zeros((RANK, TEN_DEV), f32)
    for q in range(CHUNKS):
        grad_u += jnp.dot(
            v_ranks[:, q * CHUNK : (q + 1) * CHUNK], residual(low, q), preferred_element_type=f32
        )
    gu_out[...] = grad_u.reshape(2, 32, TEN_DEV).astype(bf16)

    send(gu_out.at[1 - half], gu_in.at[2 - core], sems, 3, tok_at(1 - half, z, 1))

    @pl.when(core == 0)
    def _():
        send(gu_out.at[half], gu_in.at[0], sems, 3, tok_at(half, z, 1))

    @pl.when(core == 1)
    def _():
        mine = u_all[pl.ds(half * 32, 32)]
        wait_bytes(ua_all.at[pl.ds(0, 31)], recv_sem.at[1])
        factor = jnp.concatenate([mine[:, 0, :], mine[:, 1, :]], axis=1)
        accum = jnp.concatenate([ua_all[:, 0, :], ua_all[:, 1, :]], axis=1)
        wait_bytes(gu_in, recv_sem.at[3])
        total = gu_out[half].astype(f32) + jnp.sum(gu_in[...].astype(f32), axis=0)
        gu_z[z] = total.astype(bf16)
        each_z(lambda pz: send(gu_z.at[z], gu_z.at[z], sems, 4, tok_at(half, pz, 1)))
        wait_bytes(gu_z.at[pl.ds(0, 15)], recv_sem.at[4])
        grad = jnp.sum(gu_z[...].astype(f32), axis=0)
        accum = accum + grad * grad
        factor = factor + step_rate * grad / jnp.sqrt(accum)
        fresh[half] = factor.astype(bf16)
        for h, c in ((1 - half, 0), (1 - half, 1), (half, 0)):
            send(fresh.at[half], fresh.at[half], sems, 5, tok_at(h, z, c))
        u_rows[0] = factor
        u_rows[1] = accum
        for i in range(2):
            u_pair[i : i + 1, :] = u_rows[i, pl.ds(z, 1), :]
        send(u_pair, u_got, sems, 6, tok_at(half, z, 0))
        u_next[...] = u_rows[0, pl.ds(16 + z, 1), :]
        u_accum_next[...] = u_rows[1, pl.ds(16 + z, 1), :]
        wait_bytes(fresh.at[0], recv_sem.at[5])

    @pl.when(core == 0)
    def _():
        wait_bytes(fresh, recv_sem.at[5])

    low = fresh[...].reshape(RANK, TEN_DEV)
    framed[192:256, :] = low
    for b in range(4):
        spread[b] = jnp.dot(
            order[...], framed[192 - 64 * b : 448 - 64 * b, :], preferred_element_type=f32
        ).astype(bf16)
    for q in range(CHUNKS):
        resid = residual(low, q)
        pieces = jnp.zeros((256, 128), f32)
        for b in range(4):
            pieces += lax.dot_general(
                spread[b],
                resid[128 * b : 128 * b + 128, :],
                (((1,), (1,)), ((), ())),
                preferred_element_type=f32,
            )
        gv_out[q] = pieces.reshape(16, 16, 128).astype(bf16)
        if q in PAIRED:
            other = gv_out.at[q, pl.ds((1 - x) * 8, 8)]
            send(other, gv_x.at[PAIRED.index(q)], sems, 7 + q, ten_at(y, 1 - x))
        else:
            i = STRAIGHT.index(q)
            each_ten(lambda py, px: send(gv_out.at[q, px * 8 + py], gv_in.at[i, ten], sems, 7 + q, ten_at(py, px)))
            gv_in[i, ten] = gv_out[q, ten]
    for i, q in enumerate(PAIRED):
        wait_bytes(gv_x.at[i], recv_sem.at[7 + q])
        pair = gv_out[q, pl.ds(x * 8, 8)].astype(f32) + gv_x[i].astype(f32)
        gv_mid[i] = pair.astype(bf16)
        each_y(lambda py: send(gv_mid.at[i, py], gv_y.at[i, y], sems, 7 + CHUNKS + i, ten_at(py, x)))
        gv_y[i, y] = gv_mid[i, y]

    loads[3].wait()
    for q in STRAIGHT + PAIRED:
        if q in PAIRED:
            i = PAIRED.index(q)
            wait_bytes(gv_y.at[i, pl.ds(0, 7)], recv_sem.at[7 + CHUNKS + i])
            gv_sum[...] = jnp.sum(gv_y[i].astype(f32), axis=0)
        else:
            i = STRAIGHT.index(q)
            wait_bytes(gv_in.at[i, pl.ds(0, 15)], recv_sem.at[7 + q])
            gv_sum[...] = jnp.sum(gv_in[i].astype(f32), axis=0)
        for b in range(4):
            start = q * CHUNK + b * 128
            g_tile[:, start : start + 128] = gv_sum[4 * b : 4 * b + 4, :]
        cols = slice(q * CHUNK, min(q * CHUNK + CHUNK, TOK_DEV))
        grad = g_tile[:, cols]
        accum = va_in[:, cols] + grad * grad
        v_accum_next[:, cols] = accum
        v_next[:, cols] = v_in[:, cols] + step_rate * grad / jnp.sqrt(accum)

    wait_bytes(u_all.at[pl.ds(0, 63)], send_sem.at[0])
    wait_bytes(ua_all.at[pl.ds(0, 15)], send_sem.at[1])
    wait_bytes(v_all.at[pl.ds(0, 15)], send_sem.at[2])
    wait_bytes(gu_out.at[0], send_sem.at[3])

    @pl.when(core == 0)
    def _():
        wait_bytes(ua_row, send_sem.at[1])
        wait_bytes(gu_out.at[0], send_sem.at[3])
        wait_bytes(u_got, recv_sem.at[6])
        u_next[...] = u_got[0:1, :]
        u_accum_next[...] = u_got[1:2, :]

    @pl.when(core == 1)
    def _():
        wait_bytes(gu_z.at[pl.ds(0, 15)], send_sem.at[4])
        wait_bytes(gu_in, send_sem.at[5])
        wait_bytes(u_pair, send_sem.at[6])

    for i, q in enumerate(PAIRED):
        wait_bytes(gv_x.at[i], send_sem.at[7 + q])
        wait_bytes(gv_y.at[i, pl.ds(0, 7)], send_sem.at[7 + CHUNKS + i])
    for i, q in enumerate(STRAIGHT):
        wait_bytes(gv_in.at[i, pl.ds(0, 15)], send_sem.at[7 + q])


def store(*refs):
    copies = [
        pltpu.make_async_copy(src, dst, refs[8].at[i])
        for i, (src, dst) in enumerate(zip(refs[:4], refs[4:8]))
    ]
    for copy in copies:
        copy.start()
    for copy in copies:
        copy.wait()


def shards(counts, u_factor, u_accum, v_factor, v_accum):
    vmem = pltpu.VMEM
    results = (
        pl.pallas_call(
            kernel,
            out_shape=tuple(
                jax.ShapeDtypeStruct(like.shape, f32) for like in (u_factor, u_accum, v_factor, v_accum)
            ),
            in_specs=[pl.BlockSpec(memory_space=pl.ANY)] * 5,
            out_specs=(pl.BlockSpec(memory_space=vmem),) * 4,
            scratch_shapes=[
                vmem((TOK_DEV, TEN_DEV), jnp.int32),
                vmem((PAD, TEN_DEV), bf16),
                vmem((1, TEN_DEV), f32),
                vmem((1, TEN_DEV), f32),
                vmem((4, TOK_DEV), f32),
                vmem((4, TOK_DEV), f32),
                vmem((64, 128), f32),
                vmem((2, 128), f32),
                vmem((2, 128), f32),
                vmem((16, 64, 128), bf16),
                vmem((RANK, PAD), bf16),
                vmem((PAD, RANK), bf16),
                vmem((256, 256), bf16),
                vmem((64, 2, 128), f32),
                vmem((32, 2, 128), f32),
                vmem((2, 32, TEN_DEV), bf16),
                vmem((3, 32, TEN_DEV), bf16),
                vmem((16, 32, TEN_DEV), bf16),
                vmem((2, 32, TEN_DEV), f32),
                vmem((2, TEN_DEV), f32),
                vmem((2, TEN_DEV), f32),
                vmem((2, 32, TEN_DEV), bf16),
                vmem((448, TEN_DEV), bf16),
                vmem((4, 256, TEN_DEV), bf16),
                vmem((CHUNKS, 16, 16, 128), bf16),
                vmem((len(STRAIGHT), 16, 16, 128), bf16),
                vmem((len(PAIRED), 8, 16, 128), bf16),
                vmem((len(PAIRED), 8, 16, 128), bf16),
                vmem((len(PAIRED), 8, 16, 128), bf16),
                vmem((16, 128), f32),
                vmem((4, PAD), f32),
                pltpu.SemaphoreType.DMA((4 + CHUNKS,)),
                pltpu.SemaphoreType.DMA((7 + CHUNKS + len(PAIRED),)),
                pltpu.SemaphoreType.DMA((7 + CHUNKS + len(PAIRED),)),
            ],
            compiler_params=pltpu.CompilerParams(
                collective_id=0, has_side_effects=True, vmem_limit_bytes=40 << 20
            ),
        )(*(pltpu.with_memory_space_constraint(a, pltpu.HBM) for a in (counts.T, u_factor, u_accum, v_factor, v_accum)))
    )
    return pl.pallas_call(
        store,
        out_shape=tuple(jax.ShapeDtypeStruct(like.shape, f32) for like in results),
        in_specs=[pl.BlockSpec(memory_space=vmem)] * 4,
        out_specs=(pl.BlockSpec(memory_space=pl.ANY),) * 4,
        scratch_shapes=[pltpu.SemaphoreType.DMA((4,))],
        compiler_params=pltpu.CompilerParams(vmem_limit_bytes=1 << 20),
    )(*results)


def solution(mesh):
    return jax.shard_map(
        shards,
        mesh=mesh,
        in_specs=(
            P("ten", "tok"),
            P("tok", "ten"),
            P("tok", "ten"),
            P("ten", "tok"),
            P("ten", "tok"),
        ),
        out_specs=(P("tok", "ten"), P("tok", "ten"), P("ten", "tok"), P("ten", "tok")),
        check_vma=False,
    )
```

```python
import jax
import jax.numpy as jnp
from jax import lax
from jax.experimental import pallas as pl
from jax.experimental.pallas import tpu as pltpu
from jax.sharding import PartitionSpec as P

MESH = pl.DeviceIdType.MESH
step_rate = 0.3
RANK = 64
TEN_DEV = 256
TOK_DEV = 2004
PAD = 2048
CHUNK = 512
CHUNKS = PAD // CHUNK
PAIRED = (0, 1)
STRAIGHT = tuple(q for q in range(CHUNKS) if q not in PAIRED)
f32, bf16 = jnp.float32, jnp.bfloat16


def place():
    tok, ten = lax.axis_index("tok"), lax.axis_index("ten")
    return tok // 32, (tok // 2) % 16, tok % 2, ten // 2, ten % 2


def tok_at(half, z, core):
    return {"tok": half * 32 + z * 2 + core}


def ten_at(y, x):
    return {"ten": y * 2 + x}


def far_first(step, size):
    return size // 2 + ((step + 1) // 2) * (1 - 2 * (step % 2))


def each_z(body):
    _, z, _, _, _ = place()

    def one(step, carry):
        body((z + far_first(step, 16)) % 16)
        return carry

    lax.fori_loop(0, 15, one, 0)


def each_quad(body):
    half, _, core, _, _ = place()
    for dh, dc in ((1, 1), (1, 0), (0, 1)):
        body((half + dh) % 2, (core + dc) % 2)


def each_core(step, body):
    half, z, core, _, _ = place()
    peer_z = (z + far_first(step, 16)) % 16
    for dh, dc in ((1, 1), (1, 0), (0, 1), (0, 0)):
        body((half + dh) % 2, peer_z, (core + dc) % 2)


def each_x(step, body):
    _, _, _, y, x = place()
    peer_y = (y + far_first(step, 8)) % 8
    for dx in (1, 0):
        body(peer_y, (x + dx) % 2)


def each_tok(body):
    _, z, _, _, _ = place()

    def one(step, carry):
        each_core(step, body)
        return carry

    lax.fori_loop(0, 15, one, 0, unroll=5)
    each_quad(lambda h, c: body(h, z, c))


def each_ten(body):
    _, _, _, y, x = place()

    def one(step, carry):
        each_x(step, body)
        return carry

    lax.fori_loop(0, 7, one, 0, unroll=7)
    body(y, (x + 1) % 2)


def each_y(body):
    _, _, _, y, _ = place()

    def one(step, carry):
        body((y + far_first(step, 8)) % 8)
        return carry

    lax.fori_loop(0, 7, one, 0)


def send(src, dst, sems, phase, peer):
    send_sem, recv_sem = sems
    pltpu.make_async_remote_copy(
        src_ref=src,
        dst_ref=dst,
        send_sem=send_sem.at[phase],
        recv_sem=recv_sem.at[phase],
        device_id=peer,
        device_id_type=MESH,
    ).start()


def wait_bytes(like, sem):
    pltpu.make_async_copy(like, like, sem).wait()


def kernel(
    counts, u_factor, u_accum, v_factor, v_accum,
    u_next, u_accum_next, v_next, v_accum_next,
    cnt, weight, u_in, ua_in, v_in, va_in, v_rows, u_row, ua_row,
    v_all, v_ranks, v_half, order, u_all, ua_all,
    gu_out, gu_in, gu_z, u_rows, u_pair, u_got, fresh, framed, spread, gv_out, gv_in, gv_x, gv_mid, gv_y, gv_sum, g_tile,
    local_sem, send_sem, recv_sem,
):
    half, z, core, y, x = place()
    ten = x * 8 + y
    slot = half * 32 + core * 16 + z
    sems = (send_sem, recv_sem)

    loads = [
        pltpu.make_async_copy(src, dst, local_sem.at[i])
        for i, (src, dst) in enumerate(
            ((v_factor, v_in), (u_factor, u_in), (u_accum, ua_in), (v_accum, va_in))
        )
    ]
    for q in range(CHUNKS):
        rows = pl.ds(q * CHUNK, min(CHUNK, TOK_DEV - q * CHUNK))
        loads.append(pltpu.make_async_copy(counts.at[rows], cnt.at[rows], local_sem.at[4 + q]))
    for load in loads:
        load.start()

    barrier = pltpu.get_barrier_semaphore()

    def greet(peer):
        pl.semaphore_signal(barrier, inc=1, device_id=peer, device_id_type=MESH)

    each_tok(lambda h, pz, c: greet(tok_at(h, pz, c)))
    each_ten(lambda py, px: greet(ten_at(py, px)))

    v_rows[60:64, :] = jnp.zeros((4, 128), f32)
    loads[0].wait()
    for b in range(16):
        width = min(128, TOK_DEV - b * 128)
        v_rows[4 * b : 4 * b + 4, :width] = v_in[:, b * 128 : b * 128 + width]
    v_all[ten] = v_rows[...].astype(bf16)
    loads[1].wait()
    loads[2].wait()
    for b in range(2):
        u_row[b : b + 1, :] = u_in[:, b * 128 : b * 128 + 128]
        ua_row[b : b + 1, :] = ua_in[:, b * 128 : b * 128 + 128]
    u_all[slot] = u_row[...]

    @pl.when(core == 1)
    def _():
        ua_all[16 + z] = ua_row[...]

    pl.semaphore_wait(barrier, 78)

    def send_u(h, pz, c):
        send(u_row, u_all.at[slot], sems, 0, tok_at(h, pz, c))

    def send_v(py, px):
        send(v_all.at[ten], v_all.at[ten], sems, 2, ten_at(py, px))

    def send_both(step, carry):
        each_core(step, send_u)
        each_x(step, send_v)
        return carry

    def send_rest(step, carry):
        each_core(step, send_u)
        return carry

    lax.fori_loop(0, 7, send_both, 0)
    send_v(y, (x + 1) % 2)
    lax.fori_loop(7, 15, send_rest, 0)
    each_quad(lambda h, c: send_u(h, z, c))
    each_z(lambda pz: send(ua_row, ua_all.at[core * 16 + z], sems, 1, tok_at(half, pz, 1)))

    @pl.when(core == 0)
    def _():
        send(ua_row, ua_all.at[z], sems, 1, tok_at(half, z, 1))


    row = lax.broadcasted_iota(jnp.int32, (256, 256), 0)
    col = lax.broadcasted_iota(jnp.int32, (256, 256), 1)
    rank = ((row >> 4) & 7) * 8 + (row >> 7) * 4 + (row & 3)
    col_rank = (col & 32) + (col & 15) * 2 + ((col >> 4) & 1)
    same = (((row >> 2) & 3) == (col >> 6)) & (rank == col_rank)
    order[...] = jnp.where(same, 1.0, 0.0).astype(bf16)

    framed[...] = jnp.zeros((448, TEN_DEV), bf16)

    weight[PAD - 48 :, :] = jnp.zeros((48, TEN_DEV), bf16)
    for q in range(CHUNKS):
        loads[4 + q].wait()
        rows = slice(q * CHUNK, min(q * CHUNK + CHUNK, TOK_DEV))
        weight[rows, :] = (0.5 + 0.25 * cnt[rows, :].astype(f32)).astype(bf16)

    wait_bytes(v_all.at[pl.ds(0, 15)], recv_sem.at[2])
    for q in range(CHUNKS):
        block = v_all[:, 16 * q : 16 * q + 16, :].reshape(256, 128)
        ranks = lax.dot_general(
            order[...], block, (((0,), (0,)), ((), ())), preferred_element_type=f32
        )
        for b in range(4):
            start = q * CHUNK + b * 128
            v_ranks[:, start : start + 128] = ranks[64 * b : 64 * b + 64, :].astype(bf16)
            v_half[start : start + 128, :] = (0.5 * ranks[64 * b : 64 * b + 64, :]).T.astype(bf16)

    def residual(low, q):
        rows = slice(q * CHUNK, (q + 1) * CHUNK)
        t = jnp.tanh(jnp.dot(v_half[rows, :], low, preferred_element_type=f32))
        return (weight[rows, :].astype(f32) * (1.0 - t) - 1.0).astype(bf16)

    wait_bytes(u_all.at[pl.ds(0, 63)], recv_sem.at[0])
    u_full = jnp.concatenate([u_all[:, 0, :], u_all[:, 1, :]], axis=1)
    low = u_full.astype(bf16)
    grad_u = jnp.zeros((RANK, TEN_DEV), f32)
    for q in range(CHUNKS):
        grad_u += jnp.dot(
            v_ranks[:, q * CHUNK : (q + 1) * CHUNK], residual(low, q), preferred_element_type=f32
        )
    gu_out[...] = grad_u.reshape(2, 32, TEN_DEV).astype(bf16)

    send(gu_out.at[1 - half], gu_in.at[2 - core], sems, 3, tok_at(1 - half, z, 1))

    @pl.when(core == 0)
    def _():
        send(gu_out.at[half], gu_in.at[0], sems, 3, tok_at(half, z, 1))

    @pl.when(core == 1)
    def _():
        mine = u_all[pl.ds(half * 32, 32)]
        wait_bytes(ua_all.at[pl.ds(0, 31)], recv_sem.at[1])
        factor = jnp.concatenate([mine[:, 0, :], mine[:, 1, :]], axis=1)
        accum = jnp.concatenate([ua_all[:, 0, :], ua_all[:, 1, :]], axis=1)
        wait_bytes(gu_in, recv_sem.at[3])
        total = gu_out[half].astype(f32) + jnp.sum(gu_in[...].astype(f32), axis=0)
        gu_z[z] = total.astype(bf16)
        each_z(lambda pz: send(gu_z.at[z], gu_z.at[z], sems, 4, tok_at(half, pz, 1)))
        wait_bytes(gu_z.at[pl.ds(0, 15)], recv_sem.at[4])
        grad = jnp.sum(gu_z[...].astype(f32), axis=0)
        accum = accum + grad * grad
        factor = factor + step_rate * grad / jnp.sqrt(accum)
        fresh[half] = factor.astype(bf16)
        for h, c in ((1 - half, 0), (1 - half, 1), (half, 0)):
            send(fresh.at[half], fresh.at[half], sems, 5, tok_at(h, z, c))
        u_rows[0] = factor
        u_rows[1] = accum
        for i in range(2):
            u_pair[i : i + 1, :] = u_rows[i, pl.ds(z, 1), :]
        send(u_pair, u_got, sems, 6, tok_at(half, z, 0))
        u_next[...] = u_rows[0, pl.ds(16 + z, 1), :]
        u_accum_next[...] = u_rows[1, pl.ds(16 + z, 1), :]
        wait_bytes(fresh.at[0], recv_sem.at[5])

    @pl.when(core == 0)
    def _():
        wait_bytes(fresh, recv_sem.at[5])

    low = fresh[...].reshape(RANK, TEN_DEV)
    framed[192:256, :] = low
    for b in range(4):
        spread[b] = jnp.dot(
            order[...], framed[192 - 64 * b : 448 - 64 * b, :], preferred_element_type=f32
        ).astype(bf16)
    for q in range(CHUNKS):
        resid = residual(low, q)
        pieces = jnp.zeros((256, 128), f32)
        for b in range(4):
            pieces += lax.dot_general(
                spread[b],
                resid[128 * b : 128 * b + 128, :],
                (((1,), (1,)), ((), ())),
                preferred_element_type=f32,
            )
        gv_out[q] = pieces.reshape(16, 16, 128).astype(bf16)
        if q in PAIRED:
            other = gv_out.at[q, pl.ds((1 - x) * 8, 8)]
            send(other, gv_x.at[PAIRED.index(q)], sems, 7 + q, ten_at(y, 1 - x))
        else:
            i = STRAIGHT.index(q)
            each_ten(lambda py, px: send(gv_out.at[q, px * 8 + py], gv_in.at[i, ten], sems, 7 + q, ten_at(py, px)))
            gv_in[i, ten] = gv_out[q, ten]
    for i, q in enumerate(PAIRED):
        wait_bytes(gv_x.at[i], recv_sem.at[7 + q])
        pair = gv_out[q, pl.ds(x * 8, 8)].astype(f32) + gv_x[i].astype(f32)
        gv_mid[i] = pair.astype(bf16)
        each_y(lambda py: send(gv_mid.at[i, py], gv_y.at[i, y], sems, 7 + CHUNKS + i, ten_at(py, x)))
        gv_y[i, y] = gv_mid[i, y]

    loads[3].wait()
    for q in STRAIGHT + PAIRED:
        if q in PAIRED:
            i = PAIRED.index(q)
            wait_bytes(gv_y.at[i, pl.ds(0, 7)], recv_sem.at[7 + CHUNKS + i])
            gv_sum[...] = jnp.sum(gv_y[i].astype(f32), axis=0)
        else:
            i = STRAIGHT.index(q)
            wait_bytes(gv_in.at[i, pl.ds(0, 15)], recv_sem.at[7 + q])
            gv_sum[...] = jnp.sum(gv_in[i].astype(f32), axis=0)
        for b in range(4):
            start = q * CHUNK + b * 128
            g_tile[:, start : start + 128] = gv_sum[4 * b : 4 * b + 4, :]
        cols = slice(q * CHUNK, min(q * CHUNK + CHUNK, TOK_DEV))
        grad = g_tile[:, cols]
        accum = va_in[:, cols] + grad * grad
        v_accum_next[:, cols] = accum
        v_next[:, cols] = v_in[:, cols] + step_rate * grad / jnp.sqrt(accum)

    wait_bytes(u_all.at[pl.ds(0, 63)], send_sem.at[0])
    wait_bytes(ua_all.at[pl.ds(0, 15)], send_sem.at[1])
    wait_bytes(v_all.at[pl.ds(0, 15)], send_sem.at[2])
    wait_bytes(gu_out.at[0], send_sem.at[3])

    @pl.when(core == 0)
    def _():
        wait_bytes(ua_row, send_sem.at[1])
        wait_bytes(gu_out.at[0], send_sem.at[3])
        wait_bytes(u_got, recv_sem.at[6])
        u_next[...] = u_got[0:1, :]
        u_accum_next[...] = u_got[1:2, :]

    @pl.when(core == 1)
    def _():
        wait_bytes(gu_z.at[pl.ds(0, 15)], send_sem.at[4])
        wait_bytes(gu_in, send_sem.at[5])
        wait_bytes(u_pair, send_sem.at[6])

    for i, q in enumerate(PAIRED):
        wait_bytes(gv_x.at[i], send_sem.at[7 + q])
        wait_bytes(gv_y.at[i, pl.ds(0, 7)], send_sem.at[7 + CHUNKS + i])
    for i, q in enumerate(STRAIGHT):
        wait_bytes(gv_in.at[i, pl.ds(0, 15)], send_sem.at[7 + q])


def store(*refs):
    copies = [
        pltpu.make_async_copy(src, dst, refs[8].at[i])
        for i, (src, dst) in enumerate(zip(refs[:4], refs[4:8]))
    ]
    for copy in copies:
        copy.start()
    for copy in copies:
        copy.wait()


def shards(counts, u_factor, u_accum, v_factor, v_accum):
    vmem = pltpu.VMEM
    results = (
        pl.pallas_call(
            kernel,
            out_shape=tuple(
                jax.ShapeDtypeStruct(like.shape, f32) for like in (u_factor, u_accum, v_factor, v_accum)
            ),
            in_specs=[pl.BlockSpec(memory_space=pl.ANY)] * 5,
            out_specs=(pl.BlockSpec(memory_space=vmem),) * 4,
            scratch_shapes=[
                vmem((TOK_DEV, TEN_DEV), jnp.int32),
                vmem((PAD, TEN_DEV), bf16),
                vmem((1, TEN_DEV), f32),
                vmem((1, TEN_DEV), f32),
                vmem((4, TOK_DEV), f32),
                vmem((4, TOK_DEV), f32),
                vmem((64, 128), f32),
                vmem((2, 128), f32),
                vmem((2, 128), f32),
                vmem((16, 64, 128), bf16),
                vmem((RANK, PAD), bf16),
                vmem((PAD, RANK), bf16),
                vmem((256, 256), bf16),
                vmem((64, 2, 128), f32),
                vmem((32, 2, 128), f32),
                vmem((2, 32, TEN_DEV), bf16),
                vmem((3, 32, TEN_DEV), bf16),
                vmem((16, 32, TEN_DEV), bf16),
                vmem((2, 32, TEN_DEV), f32),
                vmem((2, TEN_DEV), f32),
                vmem((2, TEN_DEV), f32),
                vmem((2, 32, TEN_DEV), bf16),
                vmem((448, TEN_DEV), bf16),
                vmem((4, 256, TEN_DEV), bf16),
                vmem((CHUNKS, 16, 16, 128), bf16),
                vmem((len(STRAIGHT), 16, 16, 128), bf16),
                vmem((len(PAIRED), 8, 16, 128), bf16),
                vmem((len(PAIRED), 8, 16, 128), bf16),
                vmem((len(PAIRED), 8, 16, 128), bf16),
                vmem((16, 128), f32),
                vmem((4, PAD), f32),
                pltpu.SemaphoreType.DMA((4 + CHUNKS,)),
                pltpu.SemaphoreType.DMA((7 + CHUNKS + len(PAIRED),)),
                pltpu.SemaphoreType.DMA((7 + CHUNKS + len(PAIRED),)),
            ],
            compiler_params=pltpu.CompilerParams(
                collective_id=0, has_side_effects=True, vmem_limit_bytes=40 << 20
            ),
        )(*(pltpu.with_memory_space_constraint(a, pltpu.HBM) for a in (counts.T, u_factor, u_accum, v_factor, v_accum)))
    )
    return pl.pallas_call(
        store,
        out_shape=tuple(jax.ShapeDtypeStruct(like.shape, f32) for like in results),
        in_specs=[pl.BlockSpec(memory_space=vmem)] * 4,
        out_specs=(pl.BlockSpec(memory_space=pl.ANY),) * 4,
        scratch_shapes=[pltpu.SemaphoreType.DMA((4,))],
        compiler_params=pltpu.CompilerParams(vmem_limit_bytes=1 << 20),
    )(*results)


def solution(mesh):
    return jax.shard_map(
        shards,
        mesh=mesh,
        in_specs=(
            P("ten", "tok"),
            P("tok", "ten"),
            P("tok", "ten"),
            P("ten", "tok"),
            P("ten", "tok"),
        ),
        out_specs=(P("tok", "ten"), P("tok", "ten"), P("ten", "tok"), P("ten", "tok")),
        check_vma=False,
    )
```
